32 devices in a mesh: comp: 4 (over y, core), tile: 8 (over z, x).
Axes of the slice: x: 2, y: 2, z: 4, core: 2. Of those that a mesh axis runs over, the one named last changes fastest.
Arguments:
- atm_u: float32 [20, 65536], P(None, ('comp', 'tile')), may hold values from -30 to 30
- atm_v: float32 [20, 65536], P(None, ('comp', 'tile')), may hold values from -30 to 30
- mixing: float32 [19, 65536], P(None, ('comp', 'tile')), may hold values from 0.05 to 5
- drag_prev: float32 [65536], P(('comp', 'tile')), may hold values from 0.01 to 0.3
- spectrum: float32 [29, 36, 65536], P(None, None, ('comp', 'tile')), may hold values from 0.01 to 1
- sea_mask: int32 [65536], P(('comp', 'tile')), may hold values 0 or 1
- wave_source: int32 [65536], P(('comp', 'tile')), may hold values from 0 to 65535, as said below
- column_target: int32 [65536], P(('comp', 'tile')), may hold values from 0 to 65535, as said below
- neighbours: int32 [4, 65536], P(None, ('comp', 'tile')), may hold values from 0 to 2175, as said below
Outputs:
- u_new: float32 [20, 65536], P(None, ('comp', 'tile'))
- v_new: float32 [20, 65536], P(None, ('comp', 'tile'))
- spectrum_new: float32 [29, 36, 65536], P(None, None, ('comp', 'tile'))
- log_roughness: float32 [65536], P(('comp', 'tile'))
- stress: float32 [65536], P(('comp', 'tile'))
The draws below stay inside these ranges and needn't reach their ends.
Inputs may be any that keep to these rules, and one draw needn't show every extreme that they name: `wave_source`: every column is taken by exactly one wave slot; the slots of one device take exactly 64 columns of every device. The inverse of wave_source: column_target[wave_source[p]] = p. Indices into a tile extended by 64 slots on each side; a slot's west and south neighbours lie at most 64 slots before it, east and north at most 64 after it.
All inputs are finite; a program needn't handle non-finite values. No bound on the sum of `sea_mask` on one device may be relied on, other than what follows from the above.
Results may differ from the reference program's by a relative error of at most 0.0003.
Values sent between devices are 32-bit elements; how exact they have to be, the bound alone decides.
A program may use at most 128 MiB of HBM per device.

```python
import math
import jax
import jax.numpy as jnp
from jax import lax

NFREQ = 29
NDIR = 36
LEV = 20
HALO = 64
COLS_DEV = 2048
NCOL = 65536
NPTS = 65536
N_COMP = 4
N_TILE = 8


def relay_tables(key):
    devices = N_COMP * N_TILE
    per_peer = COLS_DEV // devices
    keys_src = jax.random.split(jax.random.fold_in(key, 11), devices)
    keys_dst = jax.random.split(jax.random.fold_in(key, 12), devices)
    local_perm = jax.vmap(lambda k: jax.random.permutation(k, COLS_DEV))(keys_src)
    slot_perm = jax.vmap(lambda k: jax.random.permutation(k, COLS_DEV))(keys_dst)
    wave_idx = jnp.arange(devices, dtype=jnp.int32)[:, None, None]
    src_idx = jnp.arange(devices, dtype=jnp.int32)[None, :, None]
    item = jnp.arange(per_peer, dtype=jnp.int32)[None, None, :]
    column = src_idx * COLS_DEV + local_perm[src_idx, wave_idx * per_peer + item]
    slot = slot_perm[wave_idx, src_idx * per_peer + item]
    flat_slot = (wave_idx * COLS_DEV + slot).reshape(-1)
    source = jnp.zeros((devices * COLS_DEV,), jnp.int32).at[flat_slot].set(column.reshape(-1).astype(jnp.int32))
    target = jnp.zeros((devices * COLS_DEV,), jnp.int32).at[source].set(jnp.arange(devices * COLS_DEV, dtype=jnp.int32))
    return (source, target)


def draw_wave_source(key, part):
    return relay_tables(key)[0]


def draw_column_target(key, part):
    return relay_tables(key)[1]


def draw_neighbours(key, part):
    key = jax.random.fold_in(key, 5)
    total = NPTS
    offsets = jax.random.randint(key, (4, total), 1, HALO + 1).astype(jnp.int32)
    local = jnp.arange(total, dtype=jnp.int32) % COLS_DEV
    first = local == 0
    last = local == COLS_DEV - 1
    west = jnp.where(first, HALO, offsets[0])
    east = jnp.where(last, HALO, offsets[1])
    center = local + HALO
    return jnp.stack([center - west, center + east, center - offsets[2], center + offsets[3]]).astype(jnp.int32)


def place_ends(entries, stream_key, least, largest):
    longest = entries.shape.index(max(entries.shape))
    spots = []
    for shift in (0, 1):
        where = [jax.random.randint(jax.random.fold_in(stream_key, axis), (), 0, length) for axis, length in enumerate(entries.shape)]
        where[longest] = (where[longest] + shift) % entries.shape[longest]
        spots.append(tuple(where))
    return entries.at[spots[0]].set(least).at[spots[1]].set(largest)


def level_of(key, dims, cuts, smallest, high):
    level, own = 1.0, jax.random.fold_in(key, 6)
    for axis_at, blocks in cuts:
        heights = jnp.exp(jax.random.uniform(jax.random.fold_in(own, axis_at), (blocks,), jnp.float32, smallest / len(cuts), high / len(cuts)))
        level = level * jnp.repeat(heights, dims[axis_at] // blocks).reshape([-1 if axis == axis_at else 1 for axis in range(len(dims))])
    return level


def gaussian(own_key, shape, scale, bound, pieces=(), held_as=jnp.bfloat16):
    entries = scale * jax.random.normal(own_key, shape, jnp.float32)
    if pieces:
        entries = entries * level_of(own_key, shape, pieces, -0.22, 0.18)
    return jnp.clip(entries, -bound, bound).astype(held_as)


def setup_inputs(seed: int = 0) -> dict:
    key_of = jax.random.split(jax.random.key(seed), 10)
    atm_u = gaussian(key_of[0], (LEV, NCOL), 5.0, 30.0, ((1, 32),), jnp.float32)
    atm_v = gaussian(key_of[1], (LEV, NCOL), 5.0, 30.0, ((1, 32),), jnp.float32)
    mixing = jnp.clip(jnp.exp(math.log(5.0) - 4.6051702 * jax.random.uniform(key_of[2], (LEV - 1, NCOL), jnp.float32) ** level_of(key_of[2], (LEV - 1, NCOL), ((1, 32),), -0.2, 0.2)), 0.05, 5.0)
    drag_prev = jnp.clip(jnp.exp(math.log(0.3) - 3.4011974 * jax.random.uniform(key_of[3], (NCOL,), jnp.float32) ** level_of(key_of[3], (NCOL,), ((0, 32),), -0.2, 0.2)), 0.01, 0.3)
    spectrum = jnp.clip(jnp.exp(math.log(1.0) - 4.6051702 * jax.random.uniform(key_of[4], (NFREQ, NDIR, NPTS), jnp.float32) ** level_of(key_of[4], (NFREQ, NDIR, NPTS), ((2, 32),), -0.2, 0.2)), 0.01, 1.0)
    sea_mask = place_ends((jax.random.randint(key_of[5], (NPTS,), 0, 4) < 3).astype(jnp.int32), jax.random.fold_in(key_of[5], 1), 0, 1)
    wave_source = draw_wave_source(jax.random.fold_in(key_of[9], 71), 0)
    column_target = draw_column_target(jax.random.fold_in(key_of[9], 71), 0)
    neighbours = draw_neighbours(jax.random.fold_in(key_of[9], 71), 0)
    return {"atm_u": atm_u, "atm_v": atm_v, "mixing": mixing, "drag_prev": drag_prev, "spectrum": spectrum, "sea_mask": sea_mask, "wave_source": wave_source, "column_target": column_target, "neighbours": neighbours}


def column_solve(old, mixing, drag):
    lev = old.shape[0]
    zero = jnp.zeros_like(old[0])
    cps = []
    dps = []
    for k in range(lev):
        above = mixing[k - 1] if k > 0 else zero
        below = mixing[k] if k < lev - 1 else zero
        diag = 1.0 + above + below
        if k == lev - 1:
            diag = diag + drag
        if k == 0:
            denom = diag
            dcur = old[k] / denom
        else:
            denom = diag - above * cps[k - 1]
            dcur = (old[k] + above * dps[k - 1]) / denom
        cps.append(-below / denom)
        dps.append(dcur)
    result = [None] * lev
    result[lev - 1] = dps[lev - 1]
    for k in range(lev - 2, -1, -1):
        result[k] = dps[k] - cps[k] * result[k + 1]
    return jnp.stack(result)

def wave_block(padded, mask, nbr, wind_u, wind_v):
    nfreq, ndir, total = padded.shape
    width = nbr.shape[1]
    rim = (total - width) // 2
    center = padded[:, :, rim:rim + width]
    west = padded[:, :, nbr[0]]
    east = padded[:, :, nbr[1]]
    south = padded[:, :, nbr[2]]
    north = padded[:, :, nbr[3]]
    freq = 0.0418 * 1.1 ** jnp.arange(nfreq, dtype=jnp.float32)
    theta = 2.0 * math.pi * (jnp.arange(ndir, dtype=jnp.float32) + 0.5) / ndir
    courant = 0.7 * freq[0] / freq
    cx = (courant[:, None] * jnp.cos(theta)[None, :])[:, :, None]
    cy = (courant[:, None] * jnp.sin(theta)[None, :])[:, :, None]
    upx = jnp.where(cx > 0, west, east)
    upy = jnp.where(cy > 0, south, north)
    moved = center - jnp.abs(cx) * (center - upx) - jnp.abs(cy) * (center - upy)
    speed = jnp.maximum(jnp.sqrt(wind_u * wind_u + wind_v * wind_v), 1.0)
    ustar0 = 0.035 * speed
    cosw = (wind_u[None, :] * jnp.cos(theta)[:, None] + wind_v[None, :] * jnp.sin(theta)[:, None]) / speed[None, :]
    sigma = (freq / freq[nfreq - 1])[:, None, None]
    gamma = jnp.maximum(0.0, 18.0 * freq[:, None, None] * ustar0[None, None, :] * cosw[None] - 1.0)
    energy = lax.optimization_barrier(jnp.mean(moved, axis=(0, 1)))
    growth = 1.0 + 0.3 * sigma * gamma - 0.5 * sigma * (energy / (1.0 + energy))[None, None, :]
    fmask = mask.astype(jnp.float32)
    new_spec = fmask[None, None, :] * moved * growth
    tau_wave = fmask * lax.optimization_barrier(jnp.mean(sigma * gamma * moved, axis=(0, 1)))
    ratio = jnp.minimum(tau_wave / (ustar0 * ustar0), 0.9)
    z0 = 0.01 / jnp.sqrt(1.0 - ratio) * ustar0 * ustar0 / 9.81 + 1.5e-05
    ustar = 0.4 * speed / jnp.log(10.0 / z0)
    return (new_spec, jnp.log(z0), ustar * ustar)

def reference(atm_u, atm_v, mixing, drag_prev, spectrum, sea_mask, wave_source, column_target, neighbours):
    devices = N_COMP * N_TILE
    u_new = column_solve(atm_u, mixing, drag_prev)
    v_new = column_solve(atm_v, mixing, drag_prev)
    wind_u = atm_u[LEV - 1][wave_source]
    wind_v = atm_v[LEV - 1][wave_source]
    blocks = spectrum.reshape(NFREQ, NDIR, devices, COLS_DEV)

    def one(dev):
        before = blocks[:, :, (dev - 1) % devices, COLS_DEV - HALO:]
        own = blocks[:, :, dev, :]
        after = blocks[:, :, (dev + 1) % devices, :HALO]
        padded = jnp.concatenate([before, own, after], axis=2)
        start = (dev * COLS_DEV).astype(jnp.int32)
        mask = lax.dynamic_slice_in_dim(sea_mask, start, COLS_DEV, 0)
        nbr = lax.dynamic_slice_in_dim(neighbours, start, COLS_DEV, 1)
        wu = lax.dynamic_slice_in_dim(wind_u, start, COLS_DEV, 0)
        wv = lax.dynamic_slice_in_dim(wind_v, start, COLS_DEV, 0)
        return wave_block(padded, mask, nbr, wu, wv)
    spec, logz, tau = lax.map(one, jnp.arange(devices, dtype=jnp.int32))
    spectrum_new = jnp.transpose(spec, (1, 2, 0, 3)).reshape(NFREQ, NDIR, NPTS)
    log_roughness = logz.reshape(-1)[column_target]
    stress = tau.reshape(-1)[column_target]
    return (u_new, v_new, spectrum_new, log_roughness, stress)
```

```python
import math

import jax
import jax.numpy as jnp
import numpy as np
from jax import lax
from jax.experimental import pallas as pl
from jax.experimental.pallas import tpu as pltpu
from jax.sharding import PartitionSpec as P

HALO = 64
LANES = 128
AXES = ("comp", "tile")


def split3(value):
    first = value.astype(jnp.bfloat16)
    rest = value - first.astype(jnp.float32)
    second = rest.astype(jnp.bfloat16)
    third = (rest - second.astype(jnp.float32)).astype(jnp.bfloat16)
    return [first, second, third]


def nt_dot(a, b):
    return lax.dot_general(
        a, b, (((1,), (1,)), ((), ())), preferred_element_type=jnp.float32
    )


def one_hot(rows, index):
    iota = lax.broadcasted_iota(jnp.int32, (rows, index.shape[1]), 0)
    return jnp.where(iota == index, 1.0, 0.0)


def fill_outbox(target, values, outbox, columns):
    devices = outbox.shape[0]
    blocks = columns // LANES
    shift = int(math.log2(columns))
    hots = []
    for b in range(blocks):
        peer = lax.shift_right_logical(target[b : b + 1, :], shift)
        hots.append(one_hot(devices, peer))
    stacked = jnp.concatenate(hots, axis=0).astype(jnp.bfloat16)
    upper = jnp.where(
        lax.broadcasted_iota(jnp.int32, (LANES, LANES), 0)
        <= lax.broadcasted_iota(jnp.int32, (LANES, LANES), 1),
        1.0,
        0.0,
    ).astype(jnp.bfloat16)
    counts = jnp.dot(stacked, upper, preferred_element_type=jnp.float32)
    before = jnp.zeros((devices, 1), jnp.float32)
    total = None
    for b in range(blocks):
        hot = hots[b]
        count = counts[b * devices : (b + 1) * devices]
        rank = jnp.sum(hot * (count + before), axis=0, keepdims=True) - 1.0
        before = before + count[:, LANES - 1 :]
        place = jnp.bitwise_and(target[b : b + 1, :], columns - 1)
        high = lax.shift_right_logical(place, 7).astype(jnp.float32)
        low = jnp.bitwise_and(place, LANES - 1).astype(jnp.float32)
        rows = []
        for value in values:
            rows.extend(split3(hot * value[b : b + 1, :]))
        rows.append((hot * (high + 1.0)).astype(jnp.bfloat16))
        rows.append((hot * low).astype(jnp.bfloat16))
        ranks = one_hot(LANES, rank.astype(jnp.int32)).astype(jnp.bfloat16)
        part = nt_dot(jnp.concatenate(rows, axis=0), ranks)
        total = part if total is None else total + part
    piece = [total[i * devices : (i + 1) * devices] for i in range(8)]
    outbox[:, 0, :] = piece[0] + piece[1] + piece[2]
    outbox[:, 1, :] = piece[3] + piece[4] + piece[5]
    outbox[:, 2, :] = (piece[6] - 1.0) * LANES + piece[7]


def empty_inbox(inbox, blocks):
    devices = inbox.shape[0]
    total = jnp.zeros((6 * blocks, LANES), jnp.float32)
    for d in range(0, devices, 2):
        lefts, rights = [], []
        for e in (d, d + 1):
            place = inbox[e, 2:3, :].astype(jnp.int32)
            high = one_hot(blocks, lax.shift_right_arithmetic(place, 7))
            low = one_hot(LANES, jnp.bitwise_and(place, LANES - 1)).astype(jnp.bfloat16)
            rows = []
            for v in range(2):
                rows.extend(split3(high * inbox[e, v : v + 1, :]))
            lefts.append(jnp.concatenate(rows, axis=0))
            rights.append(low)
        total += nt_dot(jnp.concatenate(lefts, axis=1), jnp.concatenate(rights, axis=1))
    piece = [total[i * blocks : (i + 1) * blocks] for i in range(6)]
    return piece[0] + piece[1] + piece[2], piece[3] + piece[4] + piece[5]


def pack_kernel(target, first, second, outbox):
    outbox[...] = jnp.zeros_like(outbox)
    fill_outbox(target, (first, second), outbox, first.shape[0] * LANES)


def unpack_kernel(inbox, first, second):
    first[...], second[...] = empty_inbox(inbox, first.shape[0])


def solve_kernel(u_ref, v_ref, mixing, drag, u_out, v_out):
    lev = u_ref.shape[0]
    cps = []
    for k in range(lev):
        row = slice(k, k + 1)
        diag = 1.0
        if k > 0:
            above = mixing[k - 1 : k, :]
            diag = diag + above
        if k < lev - 1:
            below = mixing[row, :]
            diag = diag + below
        if k == lev - 1:
            diag = diag + drag[...]
        if k == 0:
            inverse = 1.0 / diag
            du, dv = u_ref[row, :] * inverse, v_ref[row, :] * inverse
        else:
            inverse = 1.0 / (diag - above * cps[-1])
            du = (u_ref[row, :] + above * du) * inverse
            dv = (v_ref[row, :] + above * dv) * inverse
        u_out[row, :] = du
        v_out[row, :] = dv
        if k < lev - 1:
            cps.append(below * inverse)
            cps[-1] = -cps[-1]
    for k in range(lev - 2, -1, -1):
        row = slice(k, k + 1)
        du = u_out[row, :] - cps[k] * du
        dv = v_out[row, :] - cps[k] * dv
        u_out[row, :] = du
        v_out[row, :] = dv


def rim_kernel(first, last, head, tail):
    nfreq = first.shape[0]
    half = head.shape[0]
    for f in range(half):
        lane = lax.broadcasted_iota(jnp.int32, first.shape[1:], 1)
        g = min(f + half, nfreq - 1)
        head[f] = jnp.where(lane < HALO, first[f], pltpu.roll(first[g], HALO, 1))
        tail[f] = jnp.where(lane >= HALO, last[f], pltpu.roll(last[g], HALO, 1))


def wave_kernel(
    spectrum, before, after, nbr, mask, wind_u, wind_v, spec_out, logz, tau, pad, new, sem_in, sem_out
):
    nfreq, ndir, width = spectrum.shape
    blocks = width // LANES
    half = before.shape[0]
    freq = (np.float32(0.0418) * np.float32(1.1) ** np.arange(nfreq, dtype=np.float32)).astype(np.float64)
    courant = 0.7 * freq[0] / freq
    sigma = freq / freq[-1]
    theta = 2.0 * math.pi * (np.arange(ndir) + 0.5) / ndir
    cos, sin = np.cos(theta), np.sin(theta)
    tiles = [(d, min(8, ndir - d)) for d in range(0, ndir, 8)]
    f32 = jnp.float32

    def load(c):
        lanes = pl.ds(pl.multiple_of(c * LANES, LANES), LANES)
        padded = pl.ds(pl.multiple_of(c * LANES + LANES, LANES), LANES)
        return pltpu.make_async_copy(spectrum.at[:, :, lanes], pad.at[:, :, padded], sem_in.at[c])

    def store(c):
        lanes = pl.ds(pl.multiple_of(c * LANES, LANES), LANES)
        return pltpu.make_async_copy(new.at[:, :, lanes], spec_out.at[:, :, lanes], sem_out.at[c])

    def column(values, d, n):
        iota = lax.broadcasted_iota(jnp.int32, (n, LANES), 0)
        result = jnp.full((n, LANES), float(values[d]), f32)
        for i in range(1, n):
            result = jnp.where(iota == i, float(values[d + i]), result)
        return result

    for c in range(blocks):
        load(c).start()
    for f in range(half):
        pad[f, :, 0:LANES] = before[f]
        pad[f, :, width + LANES :] = after[f]
        if f + half < nfreq:
            pad[f + half, :, 0:LANES] = pltpu.roll(before[f], HALO, 1)
            pad[f + half, :, width + LANES :] = pltpu.roll(after[f], HALO, 1)
    load(0).wait()

    def advance(j, carry):
        @pl.when(j < blocks - 1)
        def _():
            load(j + 1).wait()

        at = pl.multiple_of(j * LANES, LANES)
        here = pl.ds(at, LANES)
        west = nbr[0:1, here] - HALO - at
        east = nbr[1:2, here] - HALO - at
        south = nbr[2:3, here] - HALO - at
        north = nbr[3:4, here] - HALO - at
        wu = wind_u[pl.ds(j, 1), :]
        wv = wind_v[pl.ds(j, 1), :]
        fm = mask[pl.ds(j, 1), :].astype(f32)

        def block(shift, f, d, n):
            return pad[f, d : d + n, pl.ds(pl.multiple_of(at + shift * LANES, LANES), LANES)]

        energy = jnp.zeros((1, LANES), f32)
        push = jnp.zeros((1, LANES), f32)
        drives = []
        for d, n in tiles:
            iota = lax.broadcasted_iota(jnp.int32, (n, LANES), 0) + d

            def way(values, low, high):
                lows = [bool(values[d + i] > 0) for i in range(n)]
                if all(lows):
                    rel, pick = jnp.broadcast_to(low, (n, LANES)), 0
                elif not any(lows):
                    rel, pick = jnp.broadcast_to(high, (n, LANES)), 2
                else:
                    edge = next(i for i in range(1, n) if lows[i] != lows[0])
                    pick = (iota < d + edge) if lows[0] else (iota >= d + edge)
                    rel = jnp.where(pick, low, high)
                own = jnp.logical_and(rel >= 0, rel < LANES)
                return own, jnp.bitwise_and(rel, LANES - 1), pick

            own_x, at_x, pick_x = way(cos, west, east)
            own_y, at_y, pick_y = way(sin, south, north)
            wide = jnp.abs(column(cos, d, n))
            tall = jnp.abs(column(sin, d, n))
            drive = 0.63 * (wu * column(cos, d, n) + wv * column(sin, d, n))
            drives.append(drive)
            total = jnp.zeros((n, LANES), f32)
            total_push = jnp.zeros((n, LANES), f32)
            for f in range(nfreq):
                cell = block(1, f, d, n)

                def upwind(own, index, pick):
                    if isinstance(pick, int):
                        other = block(pick, f, d, n)
                    else:
                        other = jnp.where(pick, block(0, f, d, n), block(2, f, d, n))
                    return jnp.where(
                        own,
                        jnp.take_along_axis(cell, index, axis=1, mode="promise_in_bounds"),
                        jnp.take_along_axis(other, index, axis=1, mode="promise_in_bounds"),
                    )

                upx = upwind(own_x, at_x, pick_x)
                upy = upwind(own_y, at_y, pick_y)
                moved = cell + float(courant[f]) * (wide * (upx - cell) + tall * (upy - cell))
                new[f, d : d + n, here] = moved
                total = total + moved
                gain = jnp.maximum(0.0, float(sigma[f] * freq[f]) * drive - float(sigma[f]))
                total_push = total_push + gain * moved
            energy = energy + jnp.sum(total, axis=0, keepdims=True)
            push = push + jnp.sum(total_push, axis=0, keepdims=True)

        energy = energy / float(nfreq * ndir)
        damp = fm * (0.5 * energy / (1.0 + energy))
        speed = jnp.maximum(jnp.sqrt(wu * wu + wv * wv), 1.0)
        ustar0 = 0.035 * speed
        tau_wave = fm * (push / float(nfreq * ndir))
        ratio = jnp.minimum(tau_wave / (ustar0 * ustar0), 0.9)
        z0 = 0.01 / jnp.sqrt(1.0 - ratio) * ustar0 * ustar0 / 9.81 + 1.5e-05
        ustar = 0.4 * speed / jnp.log(10.0 / z0)
        logz[pl.ds(j, 1), :] = jnp.log(z0)
        tau[pl.ds(j, 1), :] = ustar * ustar
        for (d, n), drive in zip(tiles, drives):
            drive = drive * fm
            fmb = jnp.broadcast_to(fm, (n, LANES))
            dampb = jnp.broadcast_to(damp, (n, LANES))
            for f in range(nfreq):
                gain = jnp.maximum(
                    0.0, float(0.3 * sigma[f] * freq[f]) * drive - float(0.3 * sigma[f]) * fmb
                )
                growth = fmb - float(sigma[f]) * dampb + gain
                new[f, d : d + n, here] = new[f, d : d + n, here] * growth
        store(j).start()
        return carry

    lax.fori_loop(0, blocks, advance, 0)
    for c in range(blocks):
        store(c).wait()


VMEM = pl.BlockSpec(memory_space=pltpu.VMEM)
ANY = pl.BlockSpec(memory_space=pl.ANY)
LIMIT = 48 * 1024 * 1024


def local(
    atm_u, atm_v, mixing, drag_prev, spectrum, sea_mask, wave_source, column_target, neighbours
):
    lev, columns = atm_u.shape
    nfreq, ndir, width = spectrum.shape
    devices = lax.axis_size("comp") * lax.axis_size("tile")
    blocks = columns // LANES
    half = (nfreq + 1) // 2
    f32 = jnp.float32
    params = pltpu.CompilerParams(vmem_limit_bytes=LIMIT)
    square = jax.ShapeDtypeStruct((blocks, LANES), f32)
    box = jax.ShapeDtypeStruct((devices, 8, LANES), f32)

    rim = jax.ShapeDtypeStruct((half, ndir, LANES), f32)
    edge = lambda at: pl.BlockSpec((nfreq, ndir, LANES), lambda i: (0, 0, at))
    whole = pl.BlockSpec((half, ndir, LANES), lambda i: (0, 0, 0))
    head, tail = pl.pallas_call(
        rim_kernel,
        grid=(1,),
        in_specs=[edge(0), edge(width // LANES - 1)],
        out_specs=[whole, whole],
        out_shape=[rim, rim],
        compiler_params=params,
    )(spectrum, spectrum)
    up = [(i, (i + 1) % devices) for i in range(devices)]
    before = lax.ppermute(tail, AXES, up)
    after = lax.ppermute(head, AXES, [(b, a) for a, b in up])

    def relay(target, first, second):
        outbox = pl.pallas_call(
            pack_kernel, in_specs=[VMEM] * 3, out_specs=VMEM, out_shape=box, compiler_params=params
        )(target.reshape(blocks, LANES), first, second)
        inbox = lax.all_to_all(outbox, AXES, split_axis=0, concat_axis=0, tiled=True)
        return pl.pallas_call(
            unpack_kernel, in_specs=[VMEM], out_specs=[VMEM] * 2, out_shape=[square] * 2, compiler_params=params
        )(inbox)

    wind_u, wind_v = relay(
        column_target, atm_u[-1].reshape(blocks, LANES), atm_v[-1].reshape(blocks, LANES)
    )
    slab = jax.ShapeDtypeStruct((lev, columns), f32)
    u_new, v_new = pl.pallas_call(
        solve_kernel,
        in_specs=[VMEM] * 4,
        out_specs=[VMEM] * 2,
        out_shape=[slab, slab],
        compiler_params=params,
        cost_estimate=pl.CostEstimate(flops=20 * lev * columns, bytes_accessed=20 * lev * columns, transcendentals=0),
    )(atm_u, atm_v, mixing, drag_prev.reshape(1, columns))
    spectrum_new, logz, tau = pl.pallas_call(
        wave_kernel,
        in_specs=[ANY] + [VMEM] * 6,
        out_specs=[ANY, VMEM, VMEM],
        out_shape=[jax.ShapeDtypeStruct(spectrum.shape, f32), square, square],
        scratch_shapes=[
            pltpu.VMEM((nfreq, ndir, width + 2 * LANES), f32),
            pltpu.VMEM((nfreq, ndir, width), f32),
            pltpu.SemaphoreType.DMA((blocks,)),
            pltpu.SemaphoreType.DMA((blocks,)),
        ],
        compiler_params=params,
        cost_estimate=pl.CostEstimate(
            flops=30 * spectrum.size, bytes_accessed=8 * spectrum.size, transcendentals=0
        ),
    )(spectrum, before, after, neighbours, sea_mask.reshape(blocks, LANES), wind_u, wind_v)
    rough, stress = relay(wave_source, logz, tau)
    return (u_new, v_new, spectrum_new, rough.reshape(columns), stress.reshape(columns))


def solution(mesh):
    cols, items = P(None, AXES), P(AXES)
    cube = P(None, None, AXES)
    return jax.shard_map(
        local,
        mesh=mesh,
        in_specs=(cols, cols, cols, items, cube, items, items, items, cols),
        out_specs=(cols, cols, cube, items, items),
        check_vma=False,
    )
```

```python
import math

import jax
import jax.numpy as jnp
import numpy as np
from jax import lax
from jax.experimental import pallas as pl
from jax.experimental.pallas import tpu as pltpu
from jax.sharding import PartitionSpec as P

HALO = 64
MXU = True
LANES = 128
AXES = ("comp", "tile")


def split3(value):
    first = value.astype(jnp.bfloat16)
    rest = value - first.astype(jnp.float32)
    second = rest.astype(jnp.bfloat16)
    third = (rest - second.astype(jnp.float32)).astype(jnp.bfloat16)
    return [first, second, third]


def nt_dot(a, b):
    return lax.dot_general(
        a, b, (((1,), (1,)), ((), ())), preferred_element_type=jnp.float32
    )


def one_hot(rows, index):
    iota = lax.broadcasted_iota(jnp.int32, (rows, index.shape[1]), 0)
    return jnp.where(iota == index, 1.0, 0.0)


def fill_outbox(target, values, outbox, columns):
    devices = outbox.shape[0]
    blocks = columns // LANES
    shift = int(math.log2(columns))
    hots = []
    for b in range(blocks):
        peer = lax.shift_right_logical(target[b : b + 1, :], shift)
        hots.append(one_hot(devices, peer))
    stacked = jnp.concatenate(hots, axis=0).astype(jnp.bfloat16)
    upper = jnp.where(
        lax.broadcasted_iota(jnp.int32, (LANES, LANES), 0)
        <= lax.broadcasted_iota(jnp.int32, (LANES, LANES), 1),
        1.0,
        0.0,
    ).astype(jnp.bfloat16)
    counts = jnp.dot(stacked, upper, preferred_element_type=jnp.float32)
    before = jnp.zeros((devices, 1), jnp.float32)
    total = None
    for b in range(blocks):
        hot = hots[b]
        count = counts[b * devices : (b + 1) * devices]
        rank = jnp.sum(hot * (count + before), axis=0, keepdims=True) - 1.0
        before = before + count[:, LANES - 1 :]
        place = jnp.bitwise_and(target[b : b + 1, :], columns - 1)
        high = lax.shift_right_logical(place, 7).astype(jnp.float32)
        low = jnp.bitwise_and(place, LANES - 1).astype(jnp.float32)
        rows = []
        for value in values:
            rows.extend(split3(hot * value[b : b + 1, :]))
        rows.append((hot * (high + 1.0)).astype(jnp.bfloat16))
        rows.append((hot * low).astype(jnp.bfloat16))
        ranks = one_hot(LANES, rank.astype(jnp.int32)).astype(jnp.bfloat16)
        part = nt_dot(jnp.concatenate(rows, axis=0), ranks)
        total = part if total is None else total + part
    piece = [total[i * devices : (i + 1) * devices] for i in range(8)]
    outbox[:, 0, :] = piece[0] + piece[1] + piece[2]
    outbox[:, 1, :] = piece[3] + piece[4] + piece[5]
    outbox[:, 2, :] = (piece[6] - 1.0) * LANES + piece[7]


def empty_inbox(inbox, blocks):
    devices = inbox.shape[0]
    total = jnp.zeros((6 * blocks, LANES), jnp.float32)
    for d in range(0, devices, 2):
        lefts, rights = [], []
        for e in (d, d + 1):
            place = inbox[e, 2:3, :].astype(jnp.int32)
            high = one_hot(blocks, lax.shift_right_arithmetic(place, 7))
            low = one_hot(LANES, jnp.bitwise_and(place, LANES - 1)).astype(jnp.bfloat16)
            rows = []
            for v in range(2):
                rows.extend(split3(high * inbox[e, v : v + 1, :]))
            lefts.append(jnp.concatenate(rows, axis=0))
            rights.append(low)
        total += nt_dot(jnp.concatenate(lefts, axis=1), jnp.concatenate(rights, axis=1))
    piece = [total[i * blocks : (i + 1) * blocks] for i in range(6)]
    return piece[0] + piece[1] + piece[2], piece[3] + piece[4] + piece[5]


def pack_kernel(target, first, second, outbox):
    outbox[...] = jnp.zeros_like(outbox)
    fill_outbox(target, (first, second), outbox, first.shape[0] * LANES)


def unpack_kernel(inbox, first, second):
    first[...], second[...] = empty_inbox(inbox, first.shape[0])


def solve_kernel(u_ref, v_ref, mixing, drag, u_out, v_out):
    lev = u_ref.shape[0]
    cps = []
    for k in range(lev):
        row = slice(k, k + 1)
        diag = 1.0
        if k > 0:
            above = mixing[k - 1 : k, :]
            diag = diag + above
        if k < lev - 1:
            below = mixing[row, :]
            diag = diag + below
        if k == lev - 1:
            diag = diag + drag[...]
        if k == 0:
            inverse = 1.0 / diag
            du, dv = u_ref[row, :] * inverse, v_ref[row, :] * inverse
        else:
            inverse = 1.0 / (diag - above * cps[-1])
            du = (u_ref[row, :] + above * du) * inverse
            dv = (v_ref[row, :] + above * dv) * inverse
        u_out[row, :] = du
        v_out[row, :] = dv
        if k < lev - 1:
            cps.append(below * inverse)
            cps[-1] = -cps[-1]
    for k in range(lev - 2, -1, -1):
        row = slice(k, k + 1)
        du = u_out[row, :] - cps[k] * du
        dv = v_out[row, :] - cps[k] * dv
        u_out[row, :] = du
        v_out[row, :] = dv


def rim_kernel(first, last, head, tail):
    half = head.shape[0]
    for d in range(half):
        lane = lax.broadcasted_iota(jnp.int32, first.shape[1:], 1)
        head[d] = jnp.where(lane < HALO, first[d], pltpu.roll(first[d + half], HALO, 1))
        tail[d] = jnp.where(lane >= HALO, last[d], pltpu.roll(last[d + half], HALO, 1))


def wave_kernel(
    spectrum, before, after, nbr, mask, wind_u, wind_v, spec_out, logz, tau, pad, new, parts, sem_in, sem_out
):
    ndir, nfreq, width = spectrum.shape
    rows = parts.shape[1]
    blocks = width // LANES
    half = before.shape[0]
    quarter = ndir // 4
    theta = 2.0 * math.pi * (np.arange(ndir) + 0.5) / ndir
    cos, sin = np.cos(theta), np.sin(theta)
    f32 = jnp.float32
    spare = jnp.zeros((rows - nfreq, LANES), f32)

    def load(c):
        lanes = pl.ds(pl.multiple_of(c * LANES, LANES), LANES)
        padded = pl.ds(pl.multiple_of(c * LANES + LANES, LANES), LANES)
        return pltpu.make_async_copy(spectrum.at[:, :, lanes], pad.at[:, :, padded], sem_in.at[c])

    def store(c):
        lanes = pl.ds(pl.multiple_of(c * LANES, LANES), LANES)
        return pltpu.make_async_copy(new.at[:, :, lanes], spec_out.at[:, :, lanes], sem_out.at[c])

    def split(c):
        lanes = pl.ds(pl.multiple_of(c * LANES, LANES), LANES)
        high = pl.ds(pl.multiple_of(2 * c * LANES, LANES), LANES)
        low = pl.ds(pl.multiple_of(2 * c * LANES + LANES, LANES), LANES)
        for d in range(ndir):
            value = jnp.concatenate([pad[d, :, lanes], spare], axis=0)
            first = value.astype(jnp.bfloat16)
            parts[d, :, high] = first
            parts[d, :, low] = (value - first.astype(f32)).astype(jnp.bfloat16)

    for c in range(blocks):
        load(c).start()
    for d in range(half):
        pad[d, :, 0:LANES] = before[d]
        pad[d, :, width + LANES :] = after[d]
        pad[d + half, :, 0:LANES] = pltpu.roll(before[d], HALO, 1)
        pad[d + half, :, width + LANES :] = pltpu.roll(after[d], HALO, 1)
    if MXU:
        split(0)
        split(blocks + 1)
    load(0).wait()
    if MXU:
        split(1)

    step = lax.broadcasted_iota(jnp.int32, (nfreq, LANES), 0).astype(f32)
    scale = jnp.exp(step * math.log(1.1))
    courant = 0.7 / scale
    sigma = scale * float(1.1 ** (1 - nfreq))
    rate = sigma * scale * 0.0418

    def advance(j, carry):
        @pl.when(j < blocks - 1)
        def _():
            load(j + 1).wait()
            if MXU:
                split(j + 2)

        at = pl.multiple_of(j * LANES, LANES)
        here = pl.ds(at, LANES)
        middle = pl.ds(pl.multiple_of(at + LANES, LANES), LANES)
        rels = [nbr[i : i + 1, here] - HALO - at for i in range(4)]
        wu = wind_u[pl.ds(j, 1), :]
        wv = wind_v[pl.ds(j, 1), :]
        fm = mask[pl.ds(j, 1), :].astype(f32)

        def pick(rel, block):
            iota = lax.broadcasted_iota(jnp.int32, (LANES, LANES), 0) + block * LANES
            hot = jnp.where(iota == rel, 1.0, 0.0).astype(jnp.bfloat16)
            return jnp.concatenate([hot, hot], axis=0)

        if MXU:
            zero = jnp.zeros((2 * LANES, LANES), jnp.bfloat16)
            low_x, low_y = [pick(rels[0], b) for b in (-1, 0)], [pick(rels[2], b) for b in (-1, 0)]
            high_x, high_y = [pick(rels[1], b) for b in (0, 1)], [pick(rels[3], b) for b in (0, 1)]
            tables = [
                (0, list(zip(low_x, low_y))),
                (0, list(zip([zero] + high_x, low_y + [zero]))),
                (1, list(zip(high_x, high_y))),
                (0, list(zip(low_x + [zero], [zero] + high_y))),
            ]
            picked = []
            for q, (skip, table) in enumerate(tables):
                table = jnp.concatenate([jnp.concatenate(pair, axis=1) for pair in table], axis=0)
                lanes = pl.ds(pl.multiple_of(2 * at + 2 * LANES * skip, LANES), table.shape[0])
                window = parts[q * quarter : (q + 1) * quarter, :, lanes]
                window = window.reshape(quarter * rows, table.shape[0])
                both = jnp.dot(window, table, preferred_element_type=f32)
                picked.append(both.reshape(quarter, rows, 2 * LANES))
        else:
            full = [jnp.broadcast_to(rel, (nfreq, LANES)) for rel in rels]
            owns = [jnp.logical_and(rel >= 0, rel < LANES) for rel in full]
            index = [jnp.bitwise_and(rel, LANES - 1) for rel in full]
            left = pl.ds(at, LANES)
            right = pl.ds(pl.multiple_of(at + 2 * LANES, LANES), LANES)

        total = jnp.zeros((nfreq, LANES), f32)
        push = jnp.zeros((nfreq, LANES), f32)
        for d in range(ndir):
            cell = pad[d, :, middle]
            if MXU:
                both = picked[d // quarter][d % quarter, 0:nfreq, :]
                upx, upy = both[:, :LANES], both[:, LANES:]
            else:

                def upwind(way):
                    other = pad[d, :, right if way % 2 else left]
                    return jnp.where(
                        owns[way],
                        jnp.take_along_axis(cell, index[way], axis=1, mode="promise_in_bounds"),
                        jnp.take_along_axis(other, index[way], axis=1, mode="promise_in_bounds"),
                    )

                upx = upwind(0 if cos[d] > 0 else 1)
                upy = upwind(2 if sin[d] > 0 else 3)
            change = float(abs(cos[d])) * (upx - cell) + float(abs(sin[d])) * (upy - cell)
            moved = cell + courant * change
            new[d, :, here] = moved
            total = total + moved
            drive = 0.63 * (wu * float(cos[d]) + wv * float(sin[d]))
            push = push + jnp.maximum(0.0, rate * drive - sigma) * moved

        energy = jnp.sum(total, axis=0, keepdims=True) / float(nfreq * ndir)
        push = jnp.sum(push, axis=0, keepdims=True) / float(nfreq * ndir)
        speed = jnp.maximum(jnp.sqrt(wu * wu + wv * wv), 1.0)
        ustar0 = 0.035 * speed
        tau_wave = fm * push
        ratio = jnp.minimum(tau_wave / (ustar0 * ustar0), 0.9)
        z0 = 0.01 / jnp.sqrt(1.0 - ratio) * ustar0 * ustar0 / 9.81 + 1.5e-05
        ustar = 0.4 * speed / jnp.log(10.0 / z0)
        logz[pl.ds(j, 1), :] = jnp.log(z0)
        tau[pl.ds(j, 1), :] = ustar * ustar
        base = fm - sigma * (fm * (0.5 * energy / (1.0 + energy)))
        floor = (0.3 * sigma) * fm
        steep = 0.3 * rate
        for d in range(ndir):
            drive = fm * (0.63 * (wu * float(cos[d]) + wv * float(sin[d])))
            growth = base + jnp.maximum(0.0, steep * drive - floor)
            new[d, :, here] = new[d, :, here] * growth
        store(j).start()
        return carry

    lax.fori_loop(0, blocks, advance, 0)
    for c in range(blocks):
        store(c).wait()


VMEM = pl.BlockSpec(memory_space=pltpu.VMEM)
ANY = pl.BlockSpec(memory_space=pl.ANY)
LIMIT = 48 * 1024 * 1024


def local(
    atm_u, atm_v, mixing, drag_prev, spectrum, sea_mask, wave_source, column_target, neighbours
):
    lev, columns = atm_u.shape
    spectrum = spectrum.transpose(1, 0, 2)
    ndir, nfreq, width = spectrum.shape
    devices = lax.axis_size("comp") * lax.axis_size("tile")
    blocks = columns // LANES
    half, rows = ndir // 2, -(-nfreq // 16) * 16
    f32 = jnp.float32
    params = pltpu.CompilerParams(vmem_limit_bytes=LIMIT)
    square = jax.ShapeDtypeStruct((blocks, LANES), f32)
    box = jax.ShapeDtypeStruct((devices, 8, LANES), f32)

    rim = jax.ShapeDtypeStruct((half, nfreq, LANES), f32)
    edge = lambda at: pl.BlockSpec((ndir, nfreq, LANES), lambda i: (0, 0, at))
    whole = pl.BlockSpec((half, nfreq, LANES), lambda i: (0, 0, 0))
    head, tail = pl.pallas_call(
        rim_kernel,
        grid=(1,),
        in_specs=[edge(0), edge(width // LANES - 1)],
        out_specs=[whole, whole],
        out_shape=[rim, rim],
        compiler_params=params,
    )(spectrum, spectrum)
    up = [(i, (i + 1) % devices) for i in range(devices)]
    before = lax.ppermute(tail, AXES, up)
    after = lax.ppermute(head, AXES, [(b, a) for a, b in up])

    def relay(target, first, second):
        outbox = pl.pallas_call(
            pack_kernel, in_specs=[VMEM] * 3, out_specs=VMEM, out_shape=box, compiler_params=params
        )(target.reshape(blocks, LANES), first, second)
        inbox = lax.all_to_all(outbox, AXES, split_axis=0, concat_axis=0, tiled=True)
        return pl.pallas_call(
            unpack_kernel, in_specs=[VMEM], out_specs=[VMEM] * 2, out_shape=[square] * 2, compiler_params=params
        )(inbox)

    wind_u, wind_v = relay(
        column_target, atm_u[-1].reshape(blocks, LANES), atm_v[-1].reshape(blocks, LANES)
    )
    slab = jax.ShapeDtypeStruct((lev, columns), f32)
    u_new, v_new = pl.pallas_call(
        solve_kernel,
        in_specs=[VMEM] * 4,
        out_specs=[VMEM] * 2,
        out_shape=[slab, slab],
        compiler_params=params,
        cost_estimate=pl.CostEstimate(flops=20 * lev * columns, bytes_accessed=20 * lev * columns, transcendentals=0),
    )(atm_u, atm_v, mixing, drag_prev.reshape(1, columns))
    spectrum_new, logz, tau = pl.pallas_call(
        wave_kernel,
        in_specs=[ANY] + [VMEM] * 6,
        out_specs=[ANY, VMEM, VMEM],
        out_shape=[jax.ShapeDtypeStruct(spectrum.shape, f32), square, square],
        scratch_shapes=[
            pltpu.VMEM((ndir, nfreq, width + 2 * LANES), f32),
            pltpu.VMEM((ndir, nfreq, width), f32),
            pltpu.VMEM((ndir, rows, 2 * width + 4 * LANES), jnp.bfloat16),
            pltpu.SemaphoreType.DMA((blocks,)),
            pltpu.SemaphoreType.DMA((blocks,)),
        ],
        compiler_params=params,
        cost_estimate=pl.CostEstimate(
            flops=30 * spectrum.size, bytes_accessed=8 * spectrum.size, transcendentals=0
        ),
    )(spectrum, before, after, neighbours, sea_mask.reshape(blocks, LANES), wind_u, wind_v)
    rough, stress = relay(wave_source, logz, tau)
    spectrum_new = spectrum_new.transpose(1, 0, 2)
    return (u_new, v_new, spectrum_new, rough.reshape(columns), stress.reshape(columns))


def solution(mesh):
    cols, items = P(None, AXES), P(AXES)
    cube = P(None, None, AXES)
    return jax.shard_map(
        local,
        mesh=mesh,
        in_specs=(cols, cols, cols, items, cube, items, items, items, cols),
        out_specs=(cols, cols, cube, items, items),
        check_vma=False,
    )
```

```python
import functools
import math

import jax
import jax.numpy as jnp
import numpy as np
from jax import lax
from jax.experimental import pallas as pl
from jax.experimental.pallas import tpu as pltpu
from jax.sharding import PartitionSpec as P

HALO = 64
MXU = True
LANES = 128
AXES = ("comp", "tile")


def split3(value):
    first = value.astype(jnp.bfloat16)
    rest = value - first.astype(jnp.float32)
    second = rest.astype(jnp.bfloat16)
    third = (rest - second.astype(jnp.float32)).astype(jnp.bfloat16)
    return [first, second, third]


def nt_dot(a, b):
    return lax.dot_general(
        a, b, (((1,), (1,)), ((), ())), preferred_element_type=jnp.float32
    )


def one_hot(rows, index):
    iota = lax.broadcasted_iota(jnp.int32, (rows, index.shape[1]), 0)
    return jnp.where(iota == index, 1.0, 0.0)


def fill_outbox(target, values, outbox, columns):
    devices = outbox.shape[0]
    blocks = columns // LANES
    shift = int(math.log2(columns))
    hots = []
    for b in range(blocks):
        peer = lax.shift_right_logical(target[b : b + 1, :], shift)
        hots.append(one_hot(devices, peer))
    stacked = jnp.concatenate(hots, axis=0).astype(jnp.bfloat16)
    upper = jnp.where(
        lax.broadcasted_iota(jnp.int32, (LANES, LANES), 0)
        <= lax.broadcasted_iota(jnp.int32, (LANES, LANES), 1),
        1.0,
        0.0,
    ).astype(jnp.bfloat16)
    counts = jnp.dot(stacked, upper, preferred_element_type=jnp.float32)
    before = jnp.zeros((devices, 1), jnp.float32)
    total = None
    for b in range(blocks):
        hot = hots[b]
        count = counts[b * devices : (b + 1) * devices]
        rank = jnp.sum(hot * (count + before), axis=0, keepdims=True) - 1.0
        before = before + count[:, LANES - 1 :]
        place = jnp.bitwise_and(target[b : b + 1, :], columns - 1)
        high = lax.shift_right_logical(place, 7).astype(jnp.float32)
        low = jnp.bitwise_and(place, LANES - 1).astype(jnp.float32)
        rows = []
        for value in values:
            rows.extend(split3(hot * value[b : b + 1, :]))
        rows.append((hot * (high + 1.0)).astype(jnp.bfloat16))
        rows.append((hot * low).astype(jnp.bfloat16))
        ranks = one_hot(LANES, rank.astype(jnp.int32)).astype(jnp.bfloat16)
        part = nt_dot(jnp.concatenate(rows, axis=0), ranks)
        total = part if total is None else total + part
    piece = [total[i * devices : (i + 1) * devices] for i in range(8)]
    outbox[:, 0, :] = piece[0] + piece[1] + piece[2]
    outbox[:, 1, :] = piece[3] + piece[4] + piece[5]
    outbox[:, 2, :] = (piece[6] - 1.0) * LANES + piece[7]


def empty_inbox(inbox, blocks):
    devices = inbox.shape[0]
    total = jnp.zeros((6 * blocks, LANES), jnp.float32)
    for d in range(0, devices, 2):
        lefts, rights = [], []
        for e in (d, d + 1):
            place = inbox[e, 2:3, :].astype(jnp.int32)
            high = one_hot(blocks, lax.shift_right_arithmetic(place, 7))
            low = one_hot(LANES, jnp.bitwise_and(place, LANES - 1)).astype(jnp.bfloat16)
            rows = []
            for v in range(2):
                rows.extend(split3(high * inbox[e, v : v + 1, :]))
            lefts.append(jnp.concatenate(rows, axis=0))
            rights.append(low)
        total += nt_dot(jnp.concatenate(lefts, axis=1), jnp.concatenate(rights, axis=1))
    piece = [total[i * blocks : (i + 1) * blocks] for i in range(6)]
    return piece[0] + piece[1] + piece[2], piece[3] + piece[4] + piece[5]


def pack_kernel(target, first, second, outbox):
    outbox[...] = jnp.zeros_like(outbox)
    fill_outbox(target, (first, second), outbox, first.shape[0] * LANES)


def unpack_kernel(inbox, first, second):
    first[...], second[...] = empty_inbox(inbox, first.shape[0])


def exchange_kernel(count, tiles, *refs):
    rims = len(refs) > 4
    if rims:
        outbox, head, tail, inbox, before, after, sent, got, rim_sent, rim_got = refs
    else:
        outbox, inbox, sent, got = refs
    me = lax.axis_index("comp") * tiles + lax.axis_index("tile")

    def name(index):
        return (index // tiles, index % tiles)

    def move(source, target, send, receive, device):
        return pltpu.make_async_remote_copy(
            src_ref=source,
            dst_ref=target,
            send_sem=send,
            recv_sem=receive,
            device_id=name(device),
            device_id_type=pl.DeviceIdType.MESH,
        )

    barrier = pltpu.get_barrier_semaphore()

    def greet(step, carry):
        pl.semaphore_signal(
            barrier, inc=1, device_id=name((me + step) % count), device_id_type=pl.DeviceIdType.MESH
        )
        return carry

    lax.fori_loop(1, count, greet, 0)
    pl.semaphore_wait(barrier, count - 1)

    def start(step, carry):
        peer = (me + step) % count
        move(outbox.at[peer], inbox.at[me], sent.at[peer], got.at[me], peer).start()
        return carry

    def finish(step, carry):
        peer = (me + step) % count
        move(outbox.at[peer], inbox.at[peer], sent.at[peer], got.at[peer], peer).wait()
        return carry

    lax.fori_loop(1, count, start, 0)
    if rims:
        up = move(tail, before, rim_sent.at[0], rim_got.at[0], (me + 1) % count)
        down = move(head, after, rim_sent.at[1], rim_got.at[1], (me + count - 1) % count)
        up.start()
        down.start()
    inbox[me] = outbox[me]
    lax.fori_loop(1, count, finish, 0)
    if rims:
        up.wait()
        down.wait()


def solve_kernel(u_ref, v_ref, mixing, drag, u_out, v_out):
    lev = u_ref.shape[0]
    cps = []
    for k in range(lev):
        row = slice(k, k + 1)
        diag = 1.0
        if k > 0:
            above = mixing[k - 1 : k, :]
            diag = diag + above
        if k < lev - 1:
            below = mixing[row, :]
            diag = diag + below
        if k == lev - 1:
            diag = diag + drag[...]
        if k == 0:
            inverse = 1.0 / diag
            du, dv = u_ref[row, :] * inverse, v_ref[row, :] * inverse
        else:
            inverse = 1.0 / (diag - above * cps[-1])
            du = (u_ref[row, :] + above * du) * inverse
            dv = (v_ref[row, :] + above * dv) * inverse
        u_out[row, :] = du
        v_out[row, :] = dv
        if k < lev - 1:
            cps.append(below * inverse)
            cps[-1] = -cps[-1]
    for k in range(lev - 2, -1, -1):
        row = slice(k, k + 1)
        du = u_out[row, :] - cps[k] * du
        dv = v_out[row, :] - cps[k] * dv
        u_out[row, :] = du
        v_out[row, :] = dv


def rim_kernel(first, last, head, tail):
    half = head.shape[0]
    for d in range(half):
        lane = lax.broadcasted_iota(jnp.int32, first.shape[1:], 1)
        head[d] = jnp.where(lane < HALO, first[d], pltpu.roll(first[d + half], HALO, 1))
        tail[d] = jnp.where(lane >= HALO, last[d], pltpu.roll(last[d + half], HALO, 1))


def wave_kernel(
    spectrum, before, after, nbr, mask, wind_u, wind_v, spec_out, logz, tau, pad, new, parts, sem_in, sem_out
):
    ndir, nfreq, width = spectrum.shape
    rows = parts.shape[1]
    blocks = width // LANES
    half = before.shape[0]
    quarter = ndir // 4
    theta = 2.0 * math.pi * (np.arange(ndir) + 0.5) / ndir
    cos, sin = np.cos(theta), np.sin(theta)
    f32 = jnp.float32
    spare = jnp.zeros((rows - nfreq, LANES), f32)

    def load(c):
        lanes = pl.ds(pl.multiple_of(c * LANES, LANES), LANES)
        padded = pl.ds(pl.multiple_of(c * LANES + LANES, LANES), LANES)
        return pltpu.make_async_copy(spectrum.at[:, :, lanes], pad.at[:, :, padded], sem_in.at[c])

    def store(c):
        lanes = pl.ds(pl.multiple_of(c * LANES, LANES), LANES)
        return pltpu.make_async_copy(new.at[:, :, lanes], spec_out.at[:, :, lanes], sem_out.at[c])

    def split(c):
        lanes = pl.ds(pl.multiple_of(c * LANES, LANES), LANES)
        high = pl.ds(pl.multiple_of(2 * c * LANES, LANES), LANES)
        low = pl.ds(pl.multiple_of(2 * c * LANES + LANES, LANES), LANES)
        for d in range(ndir):
            value = jnp.concatenate([pad[d, :, lanes], spare], axis=0)
            first = value.astype(jnp.bfloat16)
            parts[d, :, high] = first
            parts[d, :, low] = (value - first.astype(f32)).astype(jnp.bfloat16)

    for c in range(blocks):
        load(c).start()
    for d in range(half):
        pad[d, :, 0:LANES] = before[d]
        pad[d, :, width + LANES :] = after[d]
        pad[d + half, :, 0:LANES] = pltpu.roll(before[d], HALO, 1)
        pad[d + half, :, width + LANES :] = pltpu.roll(after[d], HALO, 1)
    if MXU:
        split(0)
        split(blocks + 1)
    load(0).wait()
    if MXU:
        split(1)

    step = lax.broadcasted_iota(jnp.int32, (nfreq, LANES), 0).astype(f32)
    scale = jnp.exp(step * math.log(1.1))
    courant = 0.7 / scale
    sigma = scale * float(1.1 ** (1 - nfreq))
    rate = sigma * scale * 0.0418

    def advance(j, carry):
        @pl.when(j < blocks - 1)
        def _():
            load(j + 1).wait()
            if MXU:
                split(j + 2)

        at = pl.multiple_of(j * LANES, LANES)
        here = pl.ds(at, LANES)
        middle = pl.ds(pl.multiple_of(at + LANES, LANES), LANES)
        rels = [nbr[i : i + 1, here] - HALO - at for i in range(4)]
        wu = wind_u[pl.ds(j, 1), :]
        wv = wind_v[pl.ds(j, 1), :]
        fm = mask[pl.ds(j, 1), :].astype(f32)

        def pick(rel, block):
            iota = lax.broadcasted_iota(jnp.int32, (LANES, LANES), 0) + block * LANES
            hot = jnp.where(iota == rel, 1.0, 0.0).astype(jnp.bfloat16)
            return jnp.concatenate([hot, hot], axis=0)

        if MXU:
            zero = jnp.zeros((2 * LANES, LANES), jnp.bfloat16)
            low_x, low_y = [pick(rels[0], b) for b in (-1, 0)], [pick(rels[2], b) for b in (-1, 0)]
            high_x, high_y = [pick(rels[1], b) for b in (0, 1)], [pick(rels[3], b) for b in (0, 1)]
            tables = [
                (0, list(zip(low_x, low_y))),
                (0, list(zip([zero] + high_x, low_y + [zero]))),
                (1, list(zip(high_x, high_y))),
                (0, list(zip(low_x + [zero], [zero] + high_y))),
            ]
            picked = []
            for q, (skip, table) in enumerate(tables):
                table = jnp.concatenate([jnp.concatenate(pair, axis=1) for pair in table], axis=0)
                lanes = pl.ds(pl.multiple_of(2 * at + 2 * LANES * skip, LANES), table.shape[0])
                window = parts[q * quarter : (q + 1) * quarter, :, lanes]
                window = window.reshape(quarter * rows, table.shape[0])
                both = jnp.dot(window, table, preferred_element_type=f32)
                picked.append(both.reshape(quarter, rows, 2 * LANES))
        else:
            full = [jnp.broadcast_to(rel, (nfreq, LANES)) for rel in rels]
            owns = [jnp.logical_and(rel >= 0, rel < LANES) for rel in full]
            index = [jnp.bitwise_and(rel, LANES - 1) for rel in full]
            left = pl.ds(at, LANES)
            right = pl.ds(pl.multiple_of(at + 2 * LANES, LANES), LANES)

        total = jnp.zeros((nfreq, LANES), f32)
        push = jnp.zeros((nfreq, LANES), f32)
        for d in range(ndir):
            cell = pad[d, :, middle]
            if MXU:
                both = picked[d // quarter][d % quarter, 0:nfreq, :]
                upx, upy = both[:, :LANES], both[:, LANES:]
            else:

                def upwind(way):
                    other = pad[d, :, right if way % 2 else left]
                    return jnp.where(
                        owns[way],
                        jnp.take_along_axis(cell, index[way], axis=1, mode="promise_in_bounds"),
                        jnp.take_along_axis(other, index[way], axis=1, mode="promise_in_bounds"),
                    )

                upx = upwind(0 if cos[d] > 0 else 1)
                upy = upwind(2 if sin[d] > 0 else 3)
            change = float(abs(cos[d])) * (upx - cell) + float(abs(sin[d])) * (upy - cell)
            moved = cell + courant * change
            new[d, :, here] = moved
            total = total + moved
            drive = 0.63 * (wu * float(cos[d]) + wv * float(sin[d]))
            push = push + jnp.maximum(0.0, rate * drive - sigma) * moved

        energy = jnp.sum(total, axis=0, keepdims=True) / float(nfreq * ndir)
        push = jnp.sum(push, axis=0, keepdims=True) / float(nfreq * ndir)
        speed = jnp.maximum(jnp.sqrt(wu * wu + wv * wv), 1.0)
        ustar0 = 0.035 * speed
        tau_wave = fm * push
        ratio = jnp.minimum(tau_wave / (ustar0 * ustar0), 0.9)
        z0 = 0.01 / jnp.sqrt(1.0 - ratio) * ustar0 * ustar0 / 9.81 + 1.5e-05
        ustar = 0.4 * speed / jnp.log(10.0 / z0)
        logz[pl.ds(j, 1), :] = jnp.log(z0)
        tau[pl.ds(j, 1), :] = ustar * ustar
        base = fm - sigma * (fm * (0.5 * energy / (1.0 + energy)))
        floor = (0.3 * sigma) * fm
        steep = 0.3 * rate
        for d in range(ndir):
            drive = fm * (0.63 * (wu * float(cos[d]) + wv * float(sin[d])))
            growth = base + jnp.maximum(0.0, steep * drive - floor)
            new[d, :, here] = new[d, :, here] * growth
        store(j).start()
        return carry

    lax.fori_loop(0, blocks, advance, 0)
    for c in range(blocks):
        store(c).wait()


VMEM = pl.BlockSpec(memory_space=pltpu.VMEM)
ANY = pl.BlockSpec(memory_space=pl.ANY)
LIMIT = 48 * 1024 * 1024


def local(
    atm_u, atm_v, mixing, drag_prev, spectrum, sea_mask, wave_source, column_target, neighbours
):
    lev, columns = atm_u.shape
    spectrum = spectrum.transpose(1, 0, 2)
    ndir, nfreq, width = spectrum.shape
    devices = lax.axis_size("comp") * lax.axis_size("tile")
    blocks = columns // LANES
    half, rows = ndir // 2, -(-nfreq // 16) * 16
    f32 = jnp.float32
    params = pltpu.CompilerParams(vmem_limit_bytes=LIMIT)
    square = jax.ShapeDtypeStruct((blocks, LANES), f32)
    box = jax.ShapeDtypeStruct((devices, 4, LANES), f32)

    rim = jax.ShapeDtypeStruct((half, nfreq, LANES), f32)
    edge = lambda at: pl.BlockSpec((ndir, nfreq, LANES), lambda i: (0, 0, at))
    whole = pl.BlockSpec((half, nfreq, LANES), lambda i: (0, 0, 0))
    head, tail = pl.pallas_call(
        rim_kernel,
        grid=(1,),
        in_specs=[edge(0), edge(width // LANES - 1)],
        out_specs=[whole, whole],
        out_shape=[rim, rim],
        compiler_params=params,
    )(spectrum, spectrum)
    plain = dict(compiler_params=params)

    def exchange(index, box_out, *sides):
        shapes = [box] + [rim] * len(sides)
        sems = [pltpu.SemaphoreType.DMA((devices,))] * 2
        if sides:
            sems = sems + [pltpu.SemaphoreType.DMA((2,))] * 2
        return pl.pallas_call(
            functools.partial(exchange_kernel, devices, lax.axis_size("tile")),
            in_specs=[VMEM] * len(shapes),
            out_specs=[VMEM] * len(shapes),
            out_shape=shapes,
            scratch_shapes=sems,
            compiler_params=pltpu.CompilerParams(
                collective_id=index, has_side_effects=True, vmem_limit_bytes=LIMIT
            ),
        )(box_out, *sides)

    def pack(target, first, second):
        return pl.pallas_call(
            pack_kernel, in_specs=[VMEM] * 3, out_specs=VMEM, out_shape=box, **plain
        )(target.reshape(blocks, LANES), first, second)

    def unpack(inbox):
        return pl.pallas_call(
            unpack_kernel, in_specs=[VMEM], out_specs=[VMEM] * 2, out_shape=[square] * 2, **plain
        )(inbox)

    outbox = pack(column_target, atm_u[-1].reshape(blocks, LANES), atm_v[-1].reshape(blocks, LANES))
    inbox, before, after = exchange(0, outbox, head, tail)
    wind_u, wind_v = unpack(inbox)
    slab = jax.ShapeDtypeStruct((lev, columns), f32)
    u_new, v_new = pl.pallas_call(
        solve_kernel,
        in_specs=[VMEM] * 4,
        out_specs=[VMEM] * 2,
        out_shape=[slab, slab],
        compiler_params=params,
        cost_estimate=pl.CostEstimate(flops=20 * lev * columns, bytes_accessed=20 * lev * columns, transcendentals=0),
    )(atm_u, atm_v, mixing, drag_prev.reshape(1, columns))
    spectrum_new, logz, tau = pl.pallas_call(
        wave_kernel,
        in_specs=[ANY] + [VMEM] * 6,
        out_specs=[ANY, VMEM, VMEM],
        out_shape=[jax.ShapeDtypeStruct(spectrum.shape, f32), square, square],
        scratch_shapes=[
            pltpu.VMEM((ndir, nfreq, width + 2 * LANES), f32),
            pltpu.VMEM((ndir, nfreq, width), f32),
            pltpu.VMEM((ndir, rows, 2 * width + 4 * LANES), jnp.bfloat16),
            pltpu.SemaphoreType.DMA((blocks,)),
            pltpu.SemaphoreType.DMA((blocks,)),
        ],
        compiler_params=params,
        cost_estimate=pl.CostEstimate(
            flops=30 * spectrum.size, bytes_accessed=8 * spectrum.size, transcendentals=0
        ),
    )(spectrum, before, after, neighbours, sea_mask.reshape(blocks, LANES), wind_u, wind_v)
    rough, stress = unpack(exchange(1, pack(wave_source, logz, tau))[0])
    spectrum_new = spectrum_new.transpose(1, 0, 2)
    return (u_new, v_new, spectrum_new, rough.reshape(columns), stress.reshape(columns))


def solution(mesh):
    cols, items = P(None, AXES), P(AXES)
    cube = P(None, None, AXES)
    return jax.shard_map(
        local,
        mesh=mesh,
        in_specs=(cols, cols, cols, items, cube, items, items, items, cols),
        out_specs=(cols, cols, cube, items, items),
        check_vma=False,
    )
```

```python
import functools
import math

import jax
import jax.numpy as jnp
import numpy as np
from jax import lax
from jax.experimental import pallas as pl
from jax.experimental.pallas import tpu as pltpu
from jax.sharding import PartitionSpec as P

HALO = 64
MXU = True
LANES = 128
AXES = ("comp", "tile")


def split3(value):
    first = value.astype(jnp.bfloat16)
    rest = value - first.astype(jnp.float32)
    second = rest.astype(jnp.bfloat16)
    third = (rest - second.astype(jnp.float32)).astype(jnp.bfloat16)
    return [first, second, third]


def nt_dot(a, b):
    return lax.dot_general(
        a, b, (((1,), (1,)), ((), ())), preferred_element_type=jnp.float32
    )


def one_hot(rows, index):
    iota = lax.broadcasted_iota(jnp.int32, (rows, index.shape[1]), 0)
    return jnp.where(iota == index, 1.0, 0.0)


def fill_outbox(target, values, outbox, columns):
    devices = outbox.shape[0]
    blocks = columns // LANES
    shift = int(math.log2(columns))
    hots = []
    for b in range(blocks):
        peer = lax.shift_right_logical(target[b : b + 1, :], shift)
        hots.append(one_hot(devices, peer))
    stacked = jnp.concatenate(hots, axis=0).astype(jnp.bfloat16)
    upper = jnp.where(
        lax.broadcasted_iota(jnp.int32, (LANES, LANES), 0)
        <= lax.broadcasted_iota(jnp.int32, (LANES, LANES), 1),
        1.0,
        0.0,
    ).astype(jnp.bfloat16)
    counts = jnp.dot(stacked, upper, preferred_element_type=jnp.float32)
    before = jnp.zeros((devices, 1), jnp.float32)
    total = None
    for b in range(blocks):
        hot = hots[b]
        count = counts[b * devices : (b + 1) * devices]
        rank = jnp.sum(hot * (count + before), axis=0, keepdims=True) - 1.0
        before = before + count[:, LANES - 1 :]
        place = jnp.bitwise_and(target[b : b + 1, :], columns - 1)
        high = lax.shift_right_logical(place, 7).astype(jnp.float32)
        low = jnp.bitwise_and(place, LANES - 1).astype(jnp.float32)
        rows = []
        for value in values:
            rows.extend(split3(hot * value[b : b + 1, :]))
        rows.append((hot * (high + 1.0)).astype(jnp.bfloat16))
        rows.append((hot * low).astype(jnp.bfloat16))
        ranks = one_hot(LANES, rank.astype(jnp.int32)).astype(jnp.bfloat16)
        part = nt_dot(jnp.concatenate(rows, axis=0), ranks)
        total = part if total is None else total + part
    piece = [total[i * devices : (i + 1) * devices] for i in range(8)]
    outbox[:, 0, :] = piece[0] + piece[1] + piece[2]
    outbox[:, 1, :] = piece[3] + piece[4] + piece[5]
    outbox[:, 2, :] = (piece[6] - 1.0) * LANES + piece[7]


def empty_inbox(inbox, blocks):
    devices = inbox.shape[0]
    total = jnp.zeros((6 * blocks, LANES), jnp.float32)
    for d in range(0, devices, 2):
        lefts, rights = [], []
        for e in (d, d + 1):
            place = inbox[e, 2:3, :].astype(jnp.int32)
            high = one_hot(blocks, lax.shift_right_arithmetic(place, 7))
            low = one_hot(LANES, jnp.bitwise_and(place, LANES - 1)).astype(jnp.bfloat16)
            rows = []
            for v in range(2):
                rows.extend(split3(high * inbox[e, v : v + 1, :]))
            lefts.append(jnp.concatenate(rows, axis=0))
            rights.append(low)
        total += nt_dot(jnp.concatenate(lefts, axis=1), jnp.concatenate(rights, axis=1))
    piece = [total[i * blocks : (i + 1) * blocks] for i in range(6)]
    return piece[0] + piece[1] + piece[2], piece[3] + piece[4] + piece[5]


def pack_kernel(target, first, second, outbox):
    outbox[...] = jnp.zeros_like(outbox)
    fill_outbox(target, (first, second), outbox, first.shape[0] * LANES)


def unpack_kernel(inbox, first, second):
    first[...], second[...] = empty_inbox(inbox, first.shape[0])


def exchange_kernel(count, tiles, *refs):
    rims = len(refs) > 4
    if rims:
        outbox, head, tail, inbox, before, after, sent, got, rim_sent, rim_got = refs
    else:
        outbox, inbox, sent, got = refs
    me = lax.axis_index("comp") * tiles + lax.axis_index("tile")

    def name(index):
        return (index // tiles, index % tiles)

    def move(source, target, send, receive, device):
        return pltpu.make_async_remote_copy(
            src_ref=source,
            dst_ref=target,
            send_sem=send,
            recv_sem=receive,
            device_id=name(device),
            device_id_type=pl.DeviceIdType.MESH,
        )

    barrier = pltpu.get_barrier_semaphore()

    def greet(step, carry):
        pl.semaphore_signal(
            barrier, inc=1, device_id=name((me + step) % count), device_id_type=pl.DeviceIdType.MESH
        )
        return carry

    lax.fori_loop(1, count, greet, 0)
    pl.semaphore_wait(barrier, count - 1)

    def start(step, carry):
        peer = (me + step) % count
        move(outbox.at[peer], inbox.at[me], sent.at[peer], got.at[me], peer).start()
        return carry

    def finish(step, carry):
        peer = (me + step) % count
        move(outbox.at[peer], inbox.at[peer], sent.at[peer], got.at[peer], peer).wait()
        return carry

    lax.fori_loop(1, count, start, 0)
    if rims:
        up = move(tail, before, rim_sent.at[0], rim_got.at[0], (me + 1) % count)
        down = move(head, after, rim_sent.at[1], rim_got.at[1], (me + count - 1) % count)
        up.start()
        down.start()
    inbox[me] = outbox[me]
    lax.fori_loop(1, count, finish, 0)
    if rims:
        up.wait()
        down.wait()


def solve_kernel(u_ref, v_ref, mixing, drag, u_out, v_out):
    lev = u_ref.shape[0]
    cps = []
    for k in range(lev):
        row = slice(k, k + 1)
        diag = 1.0
        if k > 0:
            above = mixing[k - 1 : k, :]
            diag = diag + above
        if k < lev - 1:
            below = mixing[row, :]
            diag = diag + below
        if k == lev - 1:
            diag = diag + drag[...]
        if k == 0:
            inverse = 1.0 / diag
            du, dv = u_ref[row, :] * inverse, v_ref[row, :] * inverse
        else:
            inverse = 1.0 / (diag - above * cps[-1])
            du = (u_ref[row, :] + above * du) * inverse
            dv = (v_ref[row, :] + above * dv) * inverse
        u_out[row, :] = du
        v_out[row, :] = dv
        if k < lev - 1:
            cps.append(below * inverse)
            cps[-1] = -cps[-1]
    for k in range(lev - 2, -1, -1):
        row = slice(k, k + 1)
        du = u_out[row, :] - cps[k] * du
        dv = v_out[row, :] - cps[k] * dv
        u_out[row, :] = du
        v_out[row, :] = dv


def rim_kernel(first, last, head, tail):
    half = head.shape[0]
    for d in range(half):
        lane = lax.broadcasted_iota(jnp.int32, first.shape[1:], 1)
        head[d] = jnp.where(lane < HALO, first[d], pltpu.roll(first[d + half], HALO, 1))
        tail[d] = jnp.where(lane >= HALO, last[d], pltpu.roll(last[d + half], HALO, 1))


def wave_kernel(edge, *refs):
    if edge:
        before, after, _, *refs = refs
    spectrum, nbr, mask, wind_u, wind_v, spec_out, logz, tau, pad, new, parts, sem_in, sem_out = refs
    ndir, nfreq, width = spectrum.shape
    rows = parts.shape[1]
    blocks = width // LANES
    half = ndir // 2
    quarter = ndir // 4
    theta = 2.0 * math.pi * (np.arange(ndir) + 0.5) / ndir
    cos, sin = np.cos(theta), np.sin(theta)
    f32 = jnp.float32
    spare = jnp.zeros((rows - nfreq, LANES), f32)

    def load(c):
        lanes = pl.ds(pl.multiple_of(c * LANES, LANES), LANES)
        padded = pl.ds(pl.multiple_of(c * LANES + LANES, LANES), LANES)
        return pltpu.make_async_copy(spectrum.at[:, :, lanes], pad.at[:, :, padded], sem_in.at[c])

    def store(c):
        lanes = pl.ds(pl.multiple_of(c * LANES, LANES), LANES)
        return pltpu.make_async_copy(new.at[:, :, lanes], spec_out.at[:, :, lanes], sem_out.at[c])

    def split(c):
        lanes = pl.ds(pl.multiple_of(c * LANES, LANES), LANES)
        high = pl.ds(pl.multiple_of(2 * c * LANES, LANES), LANES)
        low = pl.ds(pl.multiple_of(2 * c * LANES + LANES, LANES), LANES)
        for d in range(ndir):
            value = jnp.concatenate([pad[d, :, lanes], spare], axis=0)
            first = value.astype(jnp.bfloat16)
            parts[d, :, high] = first
            parts[d, :, low] = (value - first.astype(f32)).astype(jnp.bfloat16)

    last = blocks - 1
    near = (0, 1, last - 1, last) if edge else range(blocks)
    for c in near:
        load(c).start()
    if edge:
        for d in range(half):
            pad[d, :, 0:LANES] = before[d]
            pad[d, :, width + LANES :] = after[d]
            pad[d + half, :, 0:LANES] = pltpu.roll(before[d], HALO, 1)
            pad[d + half, :, width + LANES :] = pltpu.roll(after[d], HALO, 1)
        split(0)
        split(blocks + 1)
    for c in near if edge else (0, 1):
        load(c).wait()
        split(c + 1)

    step = lax.broadcasted_iota(jnp.int32, (nfreq, LANES), 0).astype(f32)
    scale = jnp.exp(step * math.log(1.1))
    courant = 0.7 / scale
    sigma = scale * float(1.1 ** (1 - nfreq))
    rate = sigma * scale * 0.0418

    def advance(j, carry):
        if edge:
            j = j * last
        else:
            load(j + 1).wait()
            split(j + 2)

        at = pl.multiple_of(j * LANES, LANES)
        here = pl.ds(at, LANES)
        middle = pl.ds(pl.multiple_of(at + LANES, LANES), LANES)
        rels = [nbr[i : i + 1, here] - HALO - at for i in range(4)]
        wu = wind_u[pl.ds(j, 1), :]
        wv = wind_v[pl.ds(j, 1), :]
        fm = mask[pl.ds(j, 1), :].astype(f32)

        def pick(rel, block):
            iota = lax.broadcasted_iota(jnp.int32, (LANES, LANES), 0) + block * LANES
            hot = jnp.where(iota == rel, 1.0, 0.0).astype(jnp.bfloat16)
            return jnp.concatenate([hot, hot], axis=0)

        if MXU:
            zero = jnp.zeros((2 * LANES, LANES), jnp.bfloat16)
            low_x, low_y = [pick(rels[0], b) for b in (-1, 0)], [pick(rels[2], b) for b in (-1, 0)]
            high_x, high_y = [pick(rels[1], b) for b in (0, 1)], [pick(rels[3], b) for b in (0, 1)]
            tables = [
                (0, list(zip(low_x, low_y))),
                (0, list(zip([zero] + high_x, low_y + [zero]))),
                (1, list(zip(high_x, high_y))),
                (0, list(zip(low_x + [zero], [zero] + high_y))),
            ]
            picked = []
            for q, (skip, table) in enumerate(tables):
                table = jnp.concatenate([jnp.concatenate(pair, axis=1) for pair in table], axis=0)
                lanes = pl.ds(pl.multiple_of(2 * at + 2 * LANES * skip, LANES), table.shape[0])
                window = parts[q * quarter : (q + 1) * quarter, :, lanes]
                window = window.reshape(quarter * rows, table.shape[0])
                both = jnp.dot(window, table, preferred_element_type=f32)
                picked.append(both.reshape(quarter, rows, 2 * LANES))
        else:
            full = [jnp.broadcast_to(rel, (nfreq, LANES)) for rel in rels]
            owns = [jnp.logical_and(rel >= 0, rel < LANES) for rel in full]
            index = [jnp.bitwise_and(rel, LANES - 1) for rel in full]
            left = pl.ds(at, LANES)
            right = pl.ds(pl.multiple_of(at + 2 * LANES, LANES), LANES)

        total = jnp.zeros((nfreq, LANES), f32)
        push = jnp.zeros((nfreq, LANES), f32)
        for d in range(ndir):
            cell = pad[d, :, middle]
            if MXU:
                both = picked[d // quarter][d % quarter, 0:nfreq, :]
                upx, upy = both[:, :LANES], both[:, LANES:]
            else:

                def upwind(way):
                    other = pad[d, :, right if way % 2 else left]
                    return jnp.where(
                        owns[way],
                        jnp.take_along_axis(cell, index[way], axis=1, mode="promise_in_bounds"),
                        jnp.take_along_axis(other, index[way], axis=1, mode="promise_in_bounds"),
                    )

                upx = upwind(0 if cos[d] > 0 else 1)
                upy = upwind(2 if sin[d] > 0 else 3)
            change = float(abs(cos[d])) * (upx - cell) + float(abs(sin[d])) * (upy - cell)
            moved = cell + courant * change
            new[d, :, here] = moved
            total = total + moved
            drive = 0.63 * (wu * float(cos[d]) + wv * float(sin[d]))
            push = push + jnp.maximum(0.0, rate * drive - sigma) * moved

        energy = jnp.sum(total, axis=0, keepdims=True) / float(nfreq * ndir)
        push = jnp.sum(push, axis=0, keepdims=True) / float(nfreq * ndir)
        speed = jnp.maximum(jnp.sqrt(wu * wu + wv * wv), 1.0)
        ustar0 = 0.035 * speed
        tau_wave = fm * push
        ratio = jnp.minimum(tau_wave / (ustar0 * ustar0), 0.9)
        z0 = 0.01 / jnp.sqrt(1.0 - ratio) * ustar0 * ustar0 / 9.81 + 1.5e-05
        ustar = 0.4 * speed / jnp.log(10.0 / z0)
        logz[pl.ds(j, 1), :] = jnp.log(z0)
        tau[pl.ds(j, 1), :] = ustar * ustar
        base = fm - sigma * (fm * (0.5 * energy / (1.0 + energy)))
        floor = (0.3 * sigma) * fm
        steep = 0.3 * rate
        for d in range(ndir):
            drive = fm * (0.63 * (wu * float(cos[d]) + wv * float(sin[d])))
            growth = base + jnp.maximum(0.0, steep * drive - floor)
            new[d, :, here] = new[d, :, here] * growth
        store(j).start()
        return carry

    first, stop = (0, 2) if edge else (1, last)
    lax.fori_loop(first, stop, advance, 0)
    for c in (0, last) if edge else range(1, last):
        store(c).wait()


VMEM = pl.BlockSpec(memory_space=pltpu.VMEM)
ANY = pl.BlockSpec(memory_space=pl.ANY)
LIMIT = 48 * 1024 * 1024


def local(
    atm_u, atm_v, mixing, drag_prev, spectrum, sea_mask, wave_source, column_target, neighbours
):
    lev, columns = atm_u.shape
    spectrum = spectrum.transpose(1, 0, 2)
    ndir, nfreq, width = spectrum.shape
    devices = lax.axis_size("comp") * lax.axis_size("tile")
    blocks = columns // LANES
    half, rows = ndir // 2, -(-nfreq // 16) * 16
    f32 = jnp.float32
    params = pltpu.CompilerParams(vmem_limit_bytes=LIMIT)
    square = jax.ShapeDtypeStruct((blocks, LANES), f32)
    box = jax.ShapeDtypeStruct((devices, 4, LANES), f32)

    rim = jax.ShapeDtypeStruct((half, nfreq, LANES), f32)
    edge = lambda at: pl.BlockSpec((ndir, nfreq, LANES), lambda i: (0, 0, at))
    whole = pl.BlockSpec((half, nfreq, LANES), lambda i: (0, 0, 0))
    head, tail = pl.pallas_call(
        rim_kernel,
        grid=(1,),
        in_specs=[edge(0), edge(width // LANES - 1)],
        out_specs=[whole, whole],
        out_shape=[rim, rim],
        compiler_params=params,
    )(spectrum, spectrum)
    plain = dict(compiler_params=params)

    def exchange(index, box_out, *sides):
        shapes = [box] + [rim] * len(sides)
        sems = [pltpu.SemaphoreType.DMA((devices,))] * 2
        if sides:
            sems = sems + [pltpu.SemaphoreType.DMA((2,))] * 2
        return pl.pallas_call(
            functools.partial(exchange_kernel, devices, lax.axis_size("tile")),
            in_specs=[VMEM] * len(shapes),
            out_specs=[VMEM] * len(shapes),
            out_shape=shapes,
            scratch_shapes=sems,
            compiler_params=pltpu.CompilerParams(
                collective_id=index, has_side_effects=True, vmem_limit_bytes=LIMIT
            ),
        )(box_out, *sides)

    def pack(target, first, second):
        return pl.pallas_call(
            pack_kernel, in_specs=[VMEM] * 3, out_specs=VMEM, out_shape=box, **plain
        )(target.reshape(blocks, LANES), first, second)

    def unpack(inbox):
        return pl.pallas_call(
            unpack_kernel, in_specs=[VMEM], out_specs=[VMEM] * 2, out_shape=[square] * 2, **plain
        )(inbox)

    outbox = pack(column_target, atm_u[-1].reshape(blocks, LANES), atm_v[-1].reshape(blocks, LANES))
    (inbox,) = exchange(0, outbox)
    inbox, head, tail = lax.optimization_barrier((inbox, head, tail))
    up = [(i, (i + 1) % devices) for i in range(devices)]
    before = lax.ppermute(tail, AXES, up)
    after = lax.ppermute(head, AXES, [(b, a) for a, b in up])
    wind_u, wind_v = unpack(inbox)
    slab = jax.ShapeDtypeStruct((lev, columns), f32)
    u_new, v_new = pl.pallas_call(
        solve_kernel,
        in_specs=[VMEM] * 4,
        out_specs=[VMEM] * 2,
        out_shape=[slab, slab],
        compiler_params=params,
        cost_estimate=pl.CostEstimate(flops=20 * lev * columns, bytes_accessed=20 * lev * columns, transcendentals=0),
    )(atm_u, atm_v, mixing, drag_prev.reshape(1, columns))
    scratch = [
        pltpu.VMEM((ndir, nfreq, width + 2 * LANES), f32),
        pltpu.VMEM((ndir, nfreq, width), f32),
        pltpu.VMEM((ndir, rows, 2 * width + 4 * LANES), jnp.bfloat16),
        pltpu.SemaphoreType.DMA((blocks,)),
        pltpu.SemaphoreType.DMA((blocks,)),
    ]
    waves = [jax.ShapeDtypeStruct(spectrum.shape, f32), square, square]
    shared = (spectrum, neighbours, sea_mask.reshape(blocks, LANES), wind_u, wind_v)

    def wave(edge, *first):
        return pl.pallas_call(
            functools.partial(wave_kernel, edge),
            in_specs=[VMEM, VMEM, ANY] * edge + [ANY] + [VMEM] * 4,
            out_specs=[ANY, VMEM, VMEM],
            out_shape=waves,
            scratch_shapes=scratch,
            input_output_aliases={2: 0} if edge else {},
            cost_estimate=pl.CostEstimate(
                flops=30 * spectrum.size, bytes_accessed=8 * spectrum.size, transcendentals=0
            ),
            **plain,
        )(*first, *shared)

    inner, logz, tau = wave(False)
    spectrum_new, edge_logz, edge_tau = wave(True, before, after, inner)
    row = lax.broadcasted_iota(jnp.int32, (blocks, LANES), 0)
    inside = jnp.logical_and(row > 0, row < blocks - 1)
    logz = jnp.where(inside, logz, edge_logz)
    tau = jnp.where(inside, tau, edge_tau)
    rough, stress = unpack(exchange(1, pack(wave_source, logz, tau))[0])
    spectrum_new = spectrum_new.transpose(1, 0, 2)
    return (u_new, v_new, spectrum_new, rough.reshape(columns), stress.reshape(columns))


def solution(mesh):
    cols, items = P(None, AXES), P(AXES)
    cube = P(None, None, AXES)
    return jax.shard_map(
        local,
        mesh=mesh,
        in_specs=(cols, cols, cols, items, cube, items, items, items, cols),
        out_specs=(cols, cols, cube, items, items),
        check_vma=False,
    )
```
